1024 devices in a mesh: section: 16 (over z), expert: 16 (over y, core), seq: 4 (over x).
Axes of the slice: x: 4, y: 8, z: 16, core: 2. Of those that a mesh axis runs over, the one named last changes fastest.
Arguments:
- tokens: bfloat16 [2048, 4096], P('expert', 'section'), may hold values from -6 to 6
- route_ids: int32 [2048, 2], P('expert'), may hold values from 0 to 15, all different within a row; in each aligned block of 128 rows (0 to 127, 128 to 255, ...) at most 24 rows name the same one
- route_weights: float32 [2048, 2], P('expert'), may hold values from 0.25 to 1
- gate_weight: bfloat16 [16, 4096, 8192], P('expert', None, ('section', 'seq')), may hold values from -0.09375 to 0.09375
- up_weight: bfloat16 [16, 4096, 8192], P('expert', None, ('section', 'seq')), may hold values from -0.09375 to 0.09375
- down_weight: bfloat16 [16, 8192, 4096], P('expert', 'section', 'seq'), may hold values from -0.0625 to 0.0625
Outputs:
- mixed: bfloat16 [2048, 4096], P('expert', 'seq')
The draws below stay inside these ranges and needn't reach their ends.
Inputs may be any that keep to these rules, and one draw needn't show every extreme that they name: `route_ids`: the two ids of a token differ; among the 128 tokens of one source group (held on one index of the expert axis) no expert is named more than 24 times.
All inputs are finite; a program needn't handle non-finite values.
Results may differ from the reference program's by a relative error of at most 0.0057.
Values may be sent and summed in bfloat16 or wider, within the bound.
No kernel may reach another device: no remote copies, remote signals or barrier semaphores. Data moves between devices by JAX's collectives and lax.ppermute only.
A program may use at most 32 MiB of HBM per device.

```python
import math
import jax
import jax.numpy as jnp
import numpy as np
from jax import lax

D = 4096
FF = 8192
TOP = 2
TOK = 128
EXPERTS = 16
CAP = 24
TOKENS = 2048


def steps_of(own_key, extent, split, least, top_value):
    loudness, own = 1.0, jax.random.fold_in(own_key, 6)
    for dim, shards_of in split:
        draws = jnp.exp(jax.random.uniform(jax.random.fold_in(own, dim), (shards_of,), jnp.float32, least / len(split), top_value / len(split)))
        loudness = loudness * jnp.repeat(draws, extent[dim] // shards_of).reshape([-1 if axis == dim else 1 for axis in range(len(extent))])
    return loudness


def routed_block(stream_key, own, number, rows, amount, top, reach, slope):
    order = jax.random.permutation(stream_key, amount)
    packed, common = shares(amount, rows * top, reach, slope, True), shares(amount, rows * top, reach, slope, False)
    places = jnp.arange(amount)

    def named(lengths, turn):
        used = int((lengths > 0).sum())
        fixed = max(1, used // 4)
        passed = fixed + (places - fixed + turn * (used - fixed)) % max(1, amount - fixed)
        return jnp.zeros((amount,), jnp.int32).at[order[jnp.where(places < fixed, places, passed)]].set(jnp.asarray(lengths, jnp.int32))

    lengths = jnp.where(number % 4 == 0, named(packed, number // 4), named(common, number - number // 4 - 1))
    mixed = jax.random.permutation(jax.random.fold_in(own, 3), amount)
    donor, taker = mixed[0:amount // 2 * 2:2], mixed[1:amount // 2 * 2:2]
    room = jnp.minimum(lengths[donor] - 1, reach - lengths[taker]) // 2
    room = jnp.where((donor == order[0]) | (taker == order[0]) | (lengths[taker] == 0), 0, jnp.maximum(room, 0))
    passed = jax.random.randint(jax.random.fold_in(own, 4), (amount // 2,), 0, 1 << 20) % (room + 1)
    lengths = lengths.at[donor].add(-passed).at[taker].add(passed)
    items = jnp.searchsorted(jnp.cumsum(lengths), jnp.arange(rows * top), side="right").astype(jnp.int32)
    listing = items.reshape(top, rows).T
    listing = listing[jax.random.permutation(jax.random.fold_in(own, 1), rows)]
    turn = jax.random.randint(jax.random.fold_in(own, 2), (rows, 1), 0, top)
    return jnp.take_along_axis(listing, (jnp.arange(top)[None, :] + turn) % top, axis=1)


def shares(count, total, most, lean, full):
    loads = [(1 << 20) // math.isqrt(standing ** lean) + 1 for standing in range(1, count + 1)]
    largest = most if full else min(most, max(-(-total // count), total * loads[0] // sum(loads)))
    least = 1 if total - largest >= count - 1 else 0
    given, spare = [largest] + [least] * (count - 1), total - largest - least * (count - 1)
    while spare > 0:
        movable = [i for i in range(1, count) if given[i] < largest] or [i for i in range(1, count) if given[i] < most]
        pool, budget = sum([loads[i] for i in movable]), spare
        for i in movable:
            addition = min(most - given[i], max(1, budget * loads[i] // pool), spare)
            given[i] = given[i] + addition
            spare = spare - addition
    return np.array(given)


def gaussian(own_key, extent, width, reach, pieces=(), kind=jnp.bfloat16):
    factor_of = steps_of(own_key, extent, pieces, -0.22, 0.18) if pieces else 1.0
    array = jax.random.normal(own_key, extent, jnp.float32) * width * factor_of
    return jnp.minimum(jnp.maximum(array, -reach), reach).astype(kind)


def setup_inputs(seed: int = 0) -> dict:
    key_list = jax.random.split(jax.random.key(seed), 7)
    tokens = gaussian(key_list[0], (TOKENS, D), 1.0, 6.0, ((0, 16), (1, 16)))
    route_ids_keys = jax.random.split(jax.random.fold_in(key_list[1], 1), TOKENS // TOK)
    route_ids_turns = jax.random.permutation(jax.random.fold_in(key_list[1], 3), TOKENS // TOK)
    route_ids = jax.vmap(lambda own, number: routed_block(jax.random.fold_in(key_list[1], 2), own, number, TOK, EXPERTS, TOP, CAP, 2))(route_ids_keys, route_ids_turns).reshape((TOKENS, TOP))
    route_weights = jnp.clip(0.25 + 0.75 * jax.random.uniform(key_list[2], (TOKENS, TOP), jnp.float32) ** steps_of(key_list[2], (TOKENS, TOP), ((0, 16),), -0.2, 0.2), 0.25, 1.0)
    gate_weight = gaussian(key_list[3], (EXPERTS, D, FF), D ** -0.5, 0.09375, ((0, 16), (2, 64)))
    up_weight = gaussian(key_list[4], (EXPERTS, D, FF), D ** -0.5, 0.09375, ((0, 16), (2, 64)))
    down_weight = gaussian(key_list[5], (EXPERTS, FF, D), FF ** -0.5, 0.0625, ((0, 16), (1, 16), (2, 4)))
    return dict(tokens=tokens, route_ids=route_ids, route_weights=route_weights, gate_weight=gate_weight, up_weight=up_weight, down_weight=down_weight)


def run_expert(operands):
    expert_in, gate_block, up_block, down_block = operands
    gate = jnp.dot(expert_in, gate_block, preferred_element_type=jnp.float32)
    up = jnp.dot(expert_in, up_block, preferred_element_type=jnp.float32)
    hidden = (jax.nn.silu(gate) * up).astype(jnp.bfloat16)
    return jnp.dot(hidden, down_block, preferred_element_type=jnp.float32).astype(jnp.bfloat16)


def reference(tokens, route_ids, route_weights, gate_weight, up_weight, down_weight):
    pairs = TOKENS * TOP
    flat_ids = route_ids.reshape(-1).astype(jnp.int32)
    blocks = flat_ids.reshape(EXPERTS, TOK * TOP)
    onehot = (blocks[:, :, None] == jnp.arange(EXPERTS, dtype=jnp.int32)[None, None, :]).astype(jnp.int32)
    earlier = jnp.cumsum(onehot, axis=1) - onehot
    slot_index = jnp.sum(earlier * onehot, axis=2).reshape(-1).astype(jnp.int32)
    position = jnp.arange(pairs, dtype=jnp.int32)
    source = (position // (TOK * TOP)).astype(jnp.int32)
    row_index = (source * CAP + slot_index).astype(jnp.int32)
    token_index = (position // TOP).astype(jnp.int32)
    expert_in = jnp.zeros((EXPERTS, EXPERTS * CAP, D), tokens.dtype).at[flat_ids, row_index].set(tokens[token_index])
    expert_out = lax.map(run_expert, (expert_in, gate_weight, up_weight, down_weight))
    picked = expert_out[flat_ids, row_index].astype(jnp.float32).reshape(TOKENS, TOP, D)
    return jnp.sum(picked * route_weights[:, :, None], axis=1).astype(jnp.bfloat16)
```

```python
import functools

import jax
import jax.numpy as jnp
from jax import lax
from jax.experimental import pallas as pl
from jax.experimental.pallas import tpu as pltpu
from jax.sharding import PartitionSpec as P

VMEM = pl.BlockSpec(memory_space=pltpu.VMEM)
SMEM = pl.BlockSpec(memory_space=pltpu.SMEM)
PARAMS = pltpu.CompilerParams(vmem_limit_bytes=40 * 1024 * 1024)


def up_kernel(x_ref, w0_ref, w1_ref, w2_ref, w3_ref, own_ref, send_ref):
    sections, _, width = x_ref.shape
    for block, w_ref in enumerate((w0_ref, w1_ref, w2_ref, w3_ref)):
        total = None
        for s in range(sections):
            term = jnp.dot(
                x_ref[s], w_ref[s * width : (s + 1) * width, :], preferred_element_type=jnp.float32
            )
            total = term if total is None else total + term
        own_ref[block] = total
        send_ref[block] = total.astype(jnp.bfloat16)


def hidden_kernel(own_ref, got_ref, out_ref):
    units = out_ref.shape[2]
    for block in range(4):
        total = own_ref[block] + got_ref[block ^ 1].astype(jnp.float32)
        gate, up = total[:, :units], total[:, units:]
        out_ref[block] = (gate / (1.0 + jnp.exp(-gate)) * up).astype(jnp.bfloat16)


def down_kernel(place_ref, own_ref, got_ref, down_ref, out_ref, lhs_ref):
    rows, units = own_ref.shape[1:]
    q, b = place_ref[0], place_ref[1]
    for half, (ref, swap, turn) in enumerate(((own_ref, (0, 1, 3, 2), 0), (got_ref, (3, 2, 0, 1), 1))):
        for block in range(4):
            unit = pl.multiple_of((q ^ swap[block]) * units, units)
            lhs_ref[half, :, pl.ds(unit, units)] = ref[block]
        row = pl.multiple_of((b ^ turn) * rows, rows)
        out_ref[pl.ds(row, rows), :] = jnp.dot(
            lhs_ref[half], down_ref[...], preferred_element_type=jnp.float32
        ).astype(jnp.bfloat16)


def exchange(value, axis, flip):
    return lax.ppermute(value, axis, [(i, i ^ flip) for i in range(lax.axis_size(axis))])


def shards(tokens, route_ids, route_weights, gate_weight, up_weight, down_weight):
    experts, sections = lax.axis_size("expert"), lax.axis_size("section")
    tok_rows, top_count = route_ids.shape
    capacity = 3 * tok_rows * top_count // (2 * experts)
    rows_total = experts * capacity
    features = tokens.shape[1] // 2
    units, columns = gate_weight.shape[2], down_weight.shape[2]
    q = lax.axis_index("seq")
    a, b = (q ^ (q >> 1)) & 1, q >> 1

    def half(weight, which):
        blocks = weight[0].reshape(sections, 2, features, units)
        return jnp.where(which == 0, blocks[:, 0], blocks[:, 1]).reshape(sections * features, units)

    same = jnp.concatenate([half(gate_weight, a), half(up_weight, a)], axis=1)
    other = jnp.concatenate([half(gate_weight, 1 - a), half(up_weight, 1 - a)], axis=1)
    w1 = exchange(other, "seq", 1)
    w2 = exchange(same, "seq", 3)
    w3 = exchange(other, "seq", 2)

    flat_ids = route_ids.reshape(-1)
    pairs = tok_rows * top_count
    onehot = flat_ids[:, None] == jnp.arange(experts, dtype=jnp.int32)[None, :]
    order = jnp.arange(pairs, dtype=jnp.int32)
    below = (order[:, None] > order[None, :]).astype(jnp.bfloat16)
    earlier = jnp.dot(below, onehot.astype(jnp.bfloat16), preferred_element_type=jnp.float32)
    slot_index = jnp.sum(jnp.where(onehot, earlier, 0.0), axis=1).astype(jnp.int32)
    destination = (flat_ids * capacity + slot_index).reshape(tok_rows, top_count)
    place = jnp.arange(rows_total, dtype=jnp.int32)
    named = [destination[:, k] for k in range(top_count)]
    dispatch = sum((place[:, None] == d[None, :]).astype(jnp.bfloat16) for d in named)
    mixing = sum(
        jnp.where(d[:, None] == place[None, :], route_weights[:, k][:, None], 0.0)
        for k, d in enumerate(named)
    )
    mixing_high = mixing.astype(jnp.bfloat16)
    mixing_low = (mixing - mixing_high.astype(jnp.float32)).astype(jnp.bfloat16)

    mine = jnp.where(a == 0, tokens[:, :features], tokens[:, features:])
    outgoing = jnp.dot(dispatch, mine, preferred_element_type=jnp.float32).astype(jnp.bfloat16)
    received = lax.all_to_all(
        outgoing.reshape(experts, capacity, features), "expert", split_axis=0, concat_axis=0, tiled=True
    )
    half_rows = rows_total // 2
    kept = lax.dynamic_slice_in_dim(received.reshape(rows_total, features), b * half_rows, half_rows, 0)
    x = lax.all_gather(kept, "section", axis=0, tiled=True).reshape(sections, half_rows, features)

    own, send = pl.pallas_call(
        up_kernel,
        out_shape=(
            jax.ShapeDtypeStruct((4, half_rows, 2 * units), jnp.float32),
            jax.ShapeDtypeStruct((4, half_rows, 2 * units), jnp.bfloat16),
        ),
        in_specs=[VMEM] * 5,
        out_specs=(VMEM, VMEM),
        compiler_params=PARAMS,
    )(x, same, w1, w2, w3)
    got = exchange(send, "seq", 1)
    hidden = pl.pallas_call(
        hidden_kernel,
        out_shape=jax.ShapeDtypeStruct((4, half_rows, units), jnp.bfloat16),
        in_specs=[VMEM] * 2,
        out_specs=VMEM,
        compiler_params=PARAMS,
    )(own, got)
    other_hidden = exchange(hidden, "seq", 3)
    partial_out = pl.pallas_call(
        down_kernel,
        out_shape=jax.ShapeDtypeStruct((rows_total, columns), jnp.bfloat16),
        in_specs=[SMEM, VMEM, VMEM, VMEM],
        out_specs=VMEM,
        scratch_shapes=[pltpu.VMEM((2, half_rows, 4 * units), jnp.bfloat16)],
        compiler_params=PARAMS,
    )(jnp.stack([q, b]).astype(jnp.int32), hidden, other_hidden, down_weight[0])

    returned = lax.all_to_all(
        partial_out.reshape(experts, capacity, columns), "expert", split_axis=0, concat_axis=0, tiled=True
    ).reshape(rows_total, columns)
    mixed = jnp.dot(mixing_high, returned, preferred_element_type=jnp.float32) + jnp.dot(
        mixing_low, returned, preferred_element_type=jnp.float32
    )
    part = tok_rows // sections
    terms = lax.all_to_all(
        mixed.astype(jnp.bfloat16).reshape(sections, part, columns), "section", split_axis=0, concat_axis=0, tiled=True
    )
    summed = jnp.sum(terms.astype(jnp.float32), axis=0).astype(jnp.bfloat16)
    copies = jnp.broadcast_to(summed[None], (sections, part, columns))
    return lax.all_to_all(copies, "section", split_axis=0, concat_axis=0, tiled=True).reshape(tok_rows, columns)


def solution(mesh):
    in_specs = (
        P("expert", "section"),
        P("expert", None),
        P("expert", None),
        P("expert", None, ("section", "seq")),
        P("expert", None, ("section", "seq")),
        P("expert", "section", "seq"),
    )
    out_specs = P("expert", "seq")
    return jax.shard_map(shards, mesh=mesh, in_specs=in_specs, out_specs=out_specs, check_vma=False)
```

```python
import jax
import jax.numpy as jnp
from jax import lax
from jax.experimental import pallas as pl
from jax.experimental.pallas import tpu as pltpu
from jax.sharding import PartitionSpec as P

VMEM = pl.BlockSpec(memory_space=pltpu.VMEM)
SMEM = pl.BlockSpec(memory_space=pltpu.SMEM)
LANES = 64
PARAMS = pltpu.CompilerParams(vmem_limit_bytes=40 * 1024 * 1024)


def up_kernel(x_ref, w_ref, own_ref, send_ref):
    sections, _, width = x_ref.shape
    for block in range(w_ref.shape[0]):
        total = None
        for s in range(0, sections, 2):
            rows = jnp.concatenate([x_ref[s], x_ref[s + 1]], axis=1)
            term = jnp.dot(rows, w_ref[block, s * width : (s + 2) * width, :], preferred_element_type=jnp.float32)
            total = term if total is None else total + term
        own_ref[block] = total
        send_ref[block] = total.astype(jnp.bfloat16)


def hidden_kernel(own_ref, got_ref, out_ref):
    units = out_ref.shape[2]
    for block in range(4):
        total = own_ref[block] + got_ref[block].astype(jnp.float32)
        gate, up = total[:, :units], total[:, units:]
        out_ref[block] = (gate / (1.0 + jnp.exp(-gate)) * up).astype(jnp.bfloat16)


def down_kernel(place_ref, own_ref, got_ref, down_ref, out_ref, lhs_ref):
    units = own_ref.shape[2]
    b = place_ref[0]
    for ref, turn in ((own_ref, 0), (got_ref, 1)):
        for block in range(4):
            lhs_ref[b ^ turn, :, block * units : (block + 1) * units] = ref[block]
    top = jnp.dot(lhs_ref[0], down_ref[...], preferred_element_type=jnp.float32)
    bottom = jnp.dot(lhs_ref[1], down_ref[...], preferred_element_type=jnp.float32)
    wide = 2 * LANES
    first = lax.broadcasted_iota(jnp.int32, (top.shape[0], wide), 1) < LANES
    for block in range(top.shape[1] // wide):
        up, low = top[:, block * wide : (block + 1) * wide], bottom[:, block * wide : (block + 1) * wide]
        out_ref[2 * block] = jnp.where(first, up, pltpu.roll(low, LANES, 1)).astype(jnp.bfloat16)
        out_ref[2 * block + 1] = jnp.where(first, pltpu.roll(up, LANES, 1), low).astype(jnp.bfloat16)


def sum_kernel(terms_ref, out_ref):
    total = terms_ref[0].astype(jnp.float32)
    for s in range(1, terms_ref.shape[0]):
        total = total + terms_ref[s].astype(jnp.float32)
    total = total.astype(jnp.bfloat16)
    out_ref[0] = total
    out_ref[1] = total


def mix_kernel(place_ref, returned_ref, high_ref, low_ref, out_ref):
    rows = returned_ref[...]
    mixed = jnp.dot(high_ref[...], rows, preferred_element_type=jnp.float32) + jnp.dot(
        low_ref[...], rows, preferred_element_type=jnp.float32
    )
    half = mixed.shape[0] // 2
    turned = pltpu.roll(mixed, LANES, 1)
    first = lax.broadcasted_iota(jnp.int32, mixed.shape, 1) < LANES
    front = jnp.where(place_ref[0] == 0, mixed, turned)
    back = jnp.where(place_ref[0] == 0, turned, mixed)
    packed = jnp.where(first[:half], front[:half], back[half:]).astype(jnp.bfloat16)
    for s in range(out_ref.shape[0]):
        out_ref[s] = packed


def spread_kernel(got_ref, out_ref):
    half, wide = got_ref.shape[1:]
    first = lax.broadcasted_iota(jnp.int32, (half, wide), 1) < LANES
    for block in range(got_ref.shape[0] // 2):
        even, odd = got_ref[2 * block].astype(jnp.float32), got_ref[2 * block + 1].astype(jnp.float32)
        columns = slice(block * wide, (block + 1) * wide)
        out_ref[:half, columns] = jnp.where(first, even, pltpu.roll(odd, LANES, 1)).astype(jnp.bfloat16)
        out_ref[half:, columns] = jnp.where(first, pltpu.roll(even, LANES, 1), odd).astype(jnp.bfloat16)


def exchange(value, axis, flip):
    return lax.ppermute(value, axis, [(i, i ^ flip) for i in range(lax.axis_size(axis))])


def shards(tokens, route_ids, route_weights, gate_weight, up_weight, down_weight):
    experts, sections = lax.axis_size("expert"), lax.axis_size("section")
    tok_rows, top_count = route_ids.shape
    capacity = 3 * tok_rows * top_count // (2 * experts)
    rows_total = experts * capacity
    features = tokens.shape[1] // 2
    units, columns = gate_weight.shape[2], down_weight.shape[2]
    q = lax.axis_index("seq")
    a, b = (q ^ (q >> 1)) & 1, q >> 1

    flat_ids = route_ids.reshape(-1)
    pairs = tok_rows * top_count
    onehot = flat_ids[:, None] == jnp.arange(experts, dtype=jnp.int32)[None, :]
    order = jnp.arange(pairs, dtype=jnp.int32)
    below = (order[:, None] > order[None, :]).astype(jnp.bfloat16)
    earlier = jnp.dot(below, onehot.astype(jnp.bfloat16), preferred_element_type=jnp.float32)
    slot_index = jnp.sum(jnp.where(onehot, earlier, 0.0), axis=1).astype(jnp.int32)
    destination = (flat_ids * capacity + slot_index).reshape(tok_rows, top_count)
    place = jnp.arange(rows_total, dtype=jnp.int32)
    named = [destination[:, k] for k in range(top_count)]
    dispatch = sum((place[:, None] == d[None, :]).astype(jnp.bfloat16) for d in named)
    mixing = sum(
        jnp.where(d[:, None] == place[None, :], route_weights[:, k][:, None], 0.0)
        for k, d in enumerate(named)
    )
    mixing_high = mixing.astype(jnp.bfloat16)
    mixing_low = (mixing - mixing_high.astype(jnp.float32)).astype(jnp.bfloat16)

    mine = jnp.where(a == 0, tokens[:, :features], tokens[:, features:])
    outgoing = jnp.dot(dispatch, mine, preferred_element_type=jnp.float32).astype(jnp.bfloat16)
    outgoing, gates, ups = lax.optimization_barrier((outgoing, gate_weight, up_weight))

    def half(weight, which):
        return weight[0].reshape(sections, 2, features, units)[:, which].reshape(sections * features, units)

    halves = [jnp.concatenate([half(gates, i), half(ups, i)], axis=1) for i in range(2)]
    weights = lax.all_to_all(
        jnp.stack([halves[0], halves[1], halves[1], halves[0]]), "seq", split_axis=0, concat_axis=0, tiled=True
    )
    received = lax.all_to_all(
        outgoing.reshape(experts, capacity, features), "expert", split_axis=0, concat_axis=0, tiled=True
    )
    half_rows = rows_total // 2
    kept = lax.dynamic_slice_in_dim(received.reshape(rows_total, features), b * half_rows, half_rows, 0)
    x = lax.all_gather(kept, "section", axis=0, tiled=True).reshape(sections, half_rows, features)

    own, send = pl.pallas_call(
        up_kernel,
        out_shape=(
            jax.ShapeDtypeStruct((4, half_rows, 2 * units), jnp.float32),
            jax.ShapeDtypeStruct((4, half_rows, 2 * units), jnp.bfloat16),
        ),
        in_specs=[VMEM] * 2,
        out_specs=(VMEM, VMEM),
        compiler_params=PARAMS,
    )(x, weights)
    got = exchange(send, "seq", 1)
    hidden = pl.pallas_call(
        hidden_kernel,
        out_shape=jax.ShapeDtypeStruct((4, half_rows, units), jnp.bfloat16),
        in_specs=[VMEM] * 2,
        out_specs=VMEM,
        compiler_params=PARAMS,
    )(own, got)
    other_hidden = exchange(hidden, "seq", 3)
    pieces = pl.pallas_call(
        down_kernel,
        out_shape=jax.ShapeDtypeStruct((sections, half_rows, 2 * LANES), jnp.bfloat16),
        in_specs=[SMEM, VMEM, VMEM, VMEM],
        out_specs=VMEM,
        scratch_shapes=[pltpu.VMEM((2, half_rows, 4 * units), jnp.bfloat16)],
        compiler_params=PARAMS,
    )(b.astype(jnp.int32).reshape(1), hidden, other_hidden, down_weight[0])

    terms = lax.all_to_all(pieces, "section", split_axis=0, concat_axis=0, tiled=True)
    summed = pl.pallas_call(
        sum_kernel,
        out_shape=jax.ShapeDtypeStruct((2, half_rows, 2 * LANES), jnp.bfloat16),
        in_specs=[VMEM],
        out_specs=VMEM,
        compiler_params=PARAMS,
    )(terms)
    returned = lax.all_to_all(
        summed.reshape(experts, capacity, 2 * LANES), "expert", split_axis=0, concat_axis=0, tiled=True
    ).reshape(rows_total, 2 * LANES)
    side = (lax.axis_index("expert") // (experts // 2)).astype(jnp.int32).reshape(1)
    mixed = pl.pallas_call(
        mix_kernel,
        out_shape=jax.ShapeDtypeStruct((sections, tok_rows // 2, 2 * LANES), jnp.bfloat16),
        in_specs=[SMEM, VMEM, VMEM, VMEM],
        out_specs=VMEM,
        compiler_params=PARAMS,
    )(side, returned, mixing_high, mixing_low)
    gathered = lax.all_to_all(mixed, "section", split_axis=0, concat_axis=0, tiled=True)
    return pl.pallas_call(
        spread_kernel,
        out_shape=jax.ShapeDtypeStruct((tok_rows, columns), jnp.bfloat16),
        in_specs=[VMEM],
        out_specs=VMEM,
        compiler_params=PARAMS,
    )(gathered)


def solution(mesh):
    in_specs = (
        P("expert", "section"),
        P("expert", None),
        P("expert", None),
        P("expert", None, ("section", "seq")),
        P("expert", None, ("section", "seq")),
        P("expert", "section", "seq"),
    )
    out_specs = P("expert", "seq")
    return jax.shard_map(shards, mesh=mesh, in_specs=in_specs, out_specs=out_specs, check_vma=False)
```

```python
import jax
import jax.numpy as jnp
from jax import lax
from jax.experimental import pallas as pl
from jax.experimental.pallas import tpu as pltpu
from jax.sharding import PartitionSpec as P

VMEM = pl.BlockSpec(memory_space=pltpu.VMEM)
ANY = pl.BlockSpec(memory_space=pl.ANY)
SMEM = pl.BlockSpec(memory_space=pltpu.SMEM)
PARAMS = pltpu.CompilerParams(vmem_limit_bytes=40 * 1024 * 1024)


def split_kernel(which_ref, gate_ref, up_ref, same_ref, other_ref, sems):
    units = gate_ref.shape[3]
    copies = []
    for out_ref, turn in ((other_ref, 1), (same_ref, 0)):
        for k, ref in enumerate((gate_ref, up_ref)):
            copies.append(
                pltpu.make_async_copy(
                    ref.at[:, which_ref[0] ^ turn], out_ref.at[:, :, k * units : (k + 1) * units], sems.at[2 * turn + k]
                )
            )
    for copy in copies:
        copy.start()
    for copy in copies:
        copy.wait()


def up_kernel(x_ref, w0_ref, w1_ref, w2_ref, w3_ref, own_ref, send_ref):
    sections, _, width = x_ref.shape
    for block, w_ref in enumerate((w0_ref, w1_ref, w2_ref, w3_ref)):
        total = None
        for s in range(0, sections, 2):
            rows = jnp.concatenate([x_ref[s], x_ref[s + 1]], axis=1)
            term = jnp.dot(rows, w_ref[s * width : (s + 2) * width, :], preferred_element_type=jnp.float32)
            total = term if total is None else total + term
        own_ref[block] = total
        send_ref[block] = total.astype(jnp.bfloat16)


def hidden_kernel(own_ref, got_ref, out_ref):
    units = out_ref.shape[2]
    for block in range(4):
        total = own_ref[block] + got_ref[block ^ 1].astype(jnp.float32)
        gate, up = total[:, :units], total[:, units:]
        out_ref[block] = (gate / (1.0 + jnp.exp(-gate)) * up).astype(jnp.bfloat16)


def down_kernel(place_ref, own_ref, got_ref, down_ref, out_ref, lhs_ref):
    rows, units = own_ref.shape[1:]
    q, b = place_ref[0], place_ref[1]
    for ref, swap, turn in ((own_ref, (0, 1, 3, 2), 0), (got_ref, (3, 2, 0, 1), 1)):
        row = pl.multiple_of((b ^ turn) * rows, rows)
        for block in range(4):
            unit = pl.multiple_of((q ^ swap[block]) * units, units)
            lhs_ref[pl.ds(row, rows), pl.ds(unit, units)] = ref[block]
    out_ref[...] = jnp.dot(lhs_ref[...], down_ref[...], preferred_element_type=jnp.float32).astype(jnp.bfloat16)


def mix_kernel(returned_ref, high_ref, low_ref, out_ref):
    rows = returned_ref[...]
    out_ref[...] = (
        jnp.dot(high_ref[...], rows, preferred_element_type=jnp.float32)
        + jnp.dot(low_ref[...], rows, preferred_element_type=jnp.float32)
    ).astype(jnp.bfloat16)


def sum_kernel(terms_ref, out_ref):
    total = terms_ref[0].astype(jnp.float32)
    for s in range(1, terms_ref.shape[0]):
        total = total + terms_ref[s].astype(jnp.float32)
    total = total.astype(jnp.bfloat16)
    for s in range(out_ref.shape[0]):
        out_ref[s] = total


def exchange(value, axis, flip):
    return lax.ppermute(value, axis, [(i, i ^ flip) for i in range(lax.axis_size(axis))])


def shards(tokens, route_ids, route_weights, gate_weight, up_weight, down_weight):
    experts, sections = lax.axis_size("expert"), lax.axis_size("section")
    tok_rows, top_count = route_ids.shape
    capacity = 3 * tok_rows * top_count // (2 * experts)
    rows_total = experts * capacity
    features = tokens.shape[1] // 2
    units, columns = gate_weight.shape[2], down_weight.shape[2]
    q = lax.axis_index("seq")
    a, b = (q ^ (q >> 1)) & 1, q >> 1

    shape = jax.ShapeDtypeStruct((sections, features, 2 * units), jnp.bfloat16)
    same, other = pl.pallas_call(
        split_kernel,
        out_shape=(shape, shape),
        in_specs=[SMEM, ANY, ANY],
        out_specs=(ANY, ANY),
        scratch_shapes=[pltpu.SemaphoreType.DMA((4,))],
    )(
        a.astype(jnp.int32).reshape(1),
        gate_weight[0].reshape(sections, 2, features, units),
        up_weight[0].reshape(sections, 2, features, units),
    )
    same, other = (w.reshape(sections * features, 2 * units) for w in (same, other))
    w1 = exchange(other, "seq", 1)
    w2 = exchange(same, "seq", 3)
    w3 = exchange(other, "seq", 2)

    flat_ids = route_ids.reshape(-1)
    pairs = tok_rows * top_count
    onehot = flat_ids[:, None] == jnp.arange(experts, dtype=jnp.int32)[None, :]
    order = jnp.arange(pairs, dtype=jnp.int32)
    below = (order[:, None] > order[None, :]).astype(jnp.bfloat16)
    earlier = jnp.dot(below, onehot.astype(jnp.bfloat16), preferred_element_type=jnp.float32)
    slot_index = jnp.sum(jnp.where(onehot, earlier, 0.0), axis=1).astype(jnp.int32)
    destination = (flat_ids * capacity + slot_index).reshape(tok_rows, top_count)
    place = jnp.arange(rows_total, dtype=jnp.int32)
    named = [destination[:, k] for k in range(top_count)]
    dispatch = sum((place[:, None] == d[None, :]).astype(jnp.bfloat16) for d in named)
    mixing = sum(
        jnp.where(d[:, None] == place[None, :], route_weights[:, k][:, None], 0.0)
        for k, d in enumerate(named)
    )
    mixing_high = mixing.astype(jnp.bfloat16)
    mixing_low = (mixing - mixing_high.astype(jnp.float32)).astype(jnp.bfloat16)

    mine = jnp.where(a == 0, tokens[:, :features], tokens[:, features:])
    outgoing = jnp.dot(dispatch, mine, preferred_element_type=jnp.float32).astype(jnp.bfloat16)
    received = lax.all_to_all(
        outgoing.reshape(experts, capacity, features), "expert", split_axis=0, concat_axis=0, tiled=True
    )
    half_rows = rows_total // 2
    kept = lax.dynamic_slice_in_dim(received.reshape(rows_total, features), b * half_rows, half_rows, 0)
    kept, mixing_high, mixing_low = lax.optimization_barrier((kept, mixing_high, mixing_low))
    x = lax.all_gather(kept, "section", axis=0, tiled=True).reshape(sections, half_rows, features)

    own, send = pl.pallas_call(
        up_kernel,
        out_shape=(
            jax.ShapeDtypeStruct((4, half_rows, 2 * units), jnp.float32),
            jax.ShapeDtypeStruct((4, half_rows, 2 * units), jnp.bfloat16),
        ),
        in_specs=[VMEM] * 5,
        out_specs=(VMEM, VMEM),
        compiler_params=PARAMS,
    )(x, same, w1, w2, w3)
    got = exchange(send, "seq", 1)
    hidden = pl.pallas_call(
        hidden_kernel,
        out_shape=jax.ShapeDtypeStruct((4, half_rows, units), jnp.bfloat16),
        in_specs=[VMEM] * 2,
        out_specs=VMEM,
        compiler_params=PARAMS,
    )(own, got)
    other_hidden = exchange(hidden, "seq", 3)
    partial_out = pl.pallas_call(
        down_kernel,
        out_shape=jax.ShapeDtypeStruct((rows_total, columns), jnp.bfloat16),
        in_specs=[SMEM, VMEM, VMEM, VMEM],
        out_specs=VMEM,
        scratch_shapes=[pltpu.VMEM((rows_total, 4 * units), jnp.bfloat16)],
        compiler_params=PARAMS,
    )(jnp.stack([q, b]).astype(jnp.int32), hidden, other_hidden, down_weight[0])

    returned = lax.all_to_all(
        partial_out.reshape(experts, capacity, columns), "expert", split_axis=0, concat_axis=0, tiled=True
    ).reshape(rows_total, columns)
    mixed = pl.pallas_call(
        mix_kernel,
        out_shape=jax.ShapeDtypeStruct((tok_rows, columns), jnp.bfloat16),
        in_specs=[VMEM] * 3,
        out_specs=VMEM,
        compiler_params=PARAMS,
    )(returned, mixing_high, mixing_low)
    part = tok_rows // sections
    terms = lax.all_to_all(
        mixed.reshape(sections, part, columns), "section", split_axis=0, concat_axis=0, tiled=True
    )
    copies = pl.pallas_call(
        sum_kernel,
        out_shape=jax.ShapeDtypeStruct((sections, part, columns), jnp.bfloat16),
        in_specs=[VMEM],
        out_specs=VMEM,
        compiler_params=PARAMS,
    )(terms)
    return lax.all_to_all(copies, "section", split_axis=0, concat_axis=0, tiled=True).reshape(tok_rows, columns)


def solution(mesh):
    in_specs = (
        P("expert", "section"),
        P("expert", None),
        P("expert", None),
        P("expert", None, ("section", "seq")),
        P("expert", None, ("section", "seq")),
        P("expert", "section", "seq"),
    )
    out_specs = P("expert", "seq")
    return jax.shard_map(shards, mesh=mesh, in_specs=in_specs, out_specs=out_specs, check_vma=False)
```

```python
import jax
import jax.numpy as jnp
from jax import lax
from jax.experimental import pallas as pl
from jax.experimental.pallas import tpu as pltpu
from jax.sharding import PartitionSpec as P

VMEM = pl.BlockSpec(memory_space=pltpu.VMEM)
ANY = pl.BlockSpec(memory_space=pl.ANY)
SMEM = pl.BlockSpec(memory_space=pltpu.SMEM)
PARAMS = pltpu.CompilerParams(vmem_limit_bytes=40 * 1024 * 1024)


def split_kernel(which_ref, gate_ref, up_ref, same_ref, other_ref, sems):
    units = gate_ref.shape[3]
    copies = []
    for out_ref, turn in ((other_ref, 1), (same_ref, 0)):
        for k, ref in enumerate((gate_ref, up_ref)):
            copies.append(
                pltpu.make_async_copy(
                    ref.at[:, which_ref[0] ^ turn], out_ref.at[:, :, k * units : (k + 1) * units], sems.at[2 * turn + k]
                )
            )
    for copy in copies:
        copy.start()
    for copy in copies:
        copy.wait()


def up_kernel(x_ref, w0_ref, w1_ref, w2_ref, w3_ref, own_ref, send_ref):
    sections, _, width = x_ref.shape
    for block, w_ref in enumerate((w0_ref, w1_ref, w2_ref, w3_ref)):
        total = None
        for s in range(0, sections, 2):
            rows = jnp.concatenate([x_ref[s], x_ref[s + 1]], axis=1)
            term = jnp.dot(rows, w_ref[s * width : (s + 2) * width, :], preferred_element_type=jnp.float32)
            total = term if total is None else total + term
        own_ref[block] = total
        send_ref[block] = total.astype(jnp.bfloat16)


def hidden_kernel(own_ref, got_ref, out_ref):
    units = out_ref.shape[2]
    for block in range(4):
        total = own_ref[block] + got_ref[block ^ 1].astype(jnp.float32)
        gate, up = total[:, :units], total[:, units:]
        out_ref[block] = (gate / (1.0 + jnp.exp(-gate)) * up).astype(jnp.bfloat16)


def down_kernel(place_ref, own_ref, got_ref, down_ref, out_ref, lhs_ref):
    rows, units = own_ref.shape[1:]
    q, b = place_ref[0], place_ref[1]
    for ref, swap, turn in ((own_ref, (0, 1, 3, 2), 0), (got_ref, (3, 2, 0, 1), 1)):
        row = pl.multiple_of((b ^ turn) * rows, rows)
        for block in range(4):
            unit = pl.multiple_of((q ^ swap[block]) * units, units)
            lhs_ref[pl.ds(row, rows), pl.ds(unit, units)] = ref[block]
    out_ref[...] = jnp.dot(lhs_ref[...], down_ref[...], preferred_element_type=jnp.float32).astype(jnp.bfloat16)


def mix_kernel(returned_ref, high_ref, low_ref, out_ref):
    rows = returned_ref[...]
    out_ref[...] = (
        jnp.dot(high_ref[...], rows, preferred_element_type=jnp.float32)
        + jnp.dot(low_ref[...], rows, preferred_element_type=jnp.float32)
    ).astype(jnp.bfloat16)


def sum_kernel(terms_ref, out_ref):
    total = terms_ref[0].astype(jnp.float32)
    for s in range(1, terms_ref.shape[0]):
        total = total + terms_ref[s].astype(jnp.float32)
    total = total.astype(jnp.bfloat16)
    for s in range(out_ref.shape[0]):
        out_ref[s] = total


def exchange(value, axis, flip):
    return lax.ppermute(value, axis, [(i, i ^ flip) for i in range(lax.axis_size(axis))])


def shards(tokens, route_ids, route_weights, gate_weight, up_weight, down_weight):
    experts, sections = lax.axis_size("expert"), lax.axis_size("section")
    tok_rows, top_count = route_ids.shape
    capacity = 3 * tok_rows * top_count // (2 * experts)
    rows_total = experts * capacity
    features = tokens.shape[1] // 2
    units, columns = gate_weight.shape[2], down_weight.shape[2]
    q = lax.axis_index("seq")
    a, b = (q ^ (q >> 1)) & 1, q >> 1

    shape = jax.ShapeDtypeStruct((sections, features, 2 * units), jnp.bfloat16)
    same, other = pl.pallas_call(
        split_kernel,
        out_shape=(shape, shape),
        in_specs=[SMEM, ANY, ANY],
        out_specs=(VMEM, VMEM),
        scratch_shapes=[pltpu.SemaphoreType.DMA((4,))],
    )(
        a.astype(jnp.int32).reshape(1),
        gate_weight[0].reshape(sections, 2, features, units),
        up_weight[0].reshape(sections, 2, features, units),
    )
    same, other = (w.reshape(sections * features, 2 * units) for w in (same, other))
    w1 = exchange(other, "seq", 1)
    w2 = exchange(same, "seq", 3)
    w3 = exchange(other, "seq", 2)

    flat_ids = route_ids.reshape(-1)
    pairs = tok_rows * top_count
    onehot = flat_ids[:, None] == jnp.arange(experts, dtype=jnp.int32)[None, :]
    order = jnp.arange(pairs, dtype=jnp.int32)
    below = (order[:, None] > order[None, :]).astype(jnp.bfloat16)
    earlier = jnp.dot(below, onehot.astype(jnp.bfloat16), preferred_element_type=jnp.float32)
    slot_index = jnp.sum(jnp.where(onehot, earlier, 0.0), axis=1).astype(jnp.int32)
    destination = (flat_ids * capacity + slot_index).reshape(tok_rows, top_count)
    place = jnp.arange(rows_total, dtype=jnp.int32)
    named = [destination[:, k] for k in range(top_count)]
    dispatch = sum((place[:, None] == d[None, :]).astype(jnp.bfloat16) for d in named)
    mixing = sum(
        jnp.where(d[:, None] == place[None, :], route_weights[:, k][:, None], 0.0)
        for k, d in enumerate(named)
    )
    mixing_high = mixing.astype(jnp.bfloat16)
    mixing_low = (mixing - mixing_high.astype(jnp.float32)).astype(jnp.bfloat16)

    mine = jnp.where(a == 0, tokens[:, :features], tokens[:, features:])
    outgoing = jnp.dot(dispatch, mine, preferred_element_type=jnp.float32).astype(jnp.bfloat16)
    received = lax.all_to_all(
        outgoing.reshape(experts, capacity, features), "expert", split_axis=0, concat_axis=0, tiled=True
    )
    half_rows = rows_total // 2
    kept = lax.dynamic_slice_in_dim(received.reshape(rows_total, features), b * half_rows, half_rows, 0)
    kept, mixing_high, mixing_low = lax.optimization_barrier((kept, mixing_high, mixing_low))
    x = lax.all_gather(kept, "section", axis=0, tiled=True).reshape(sections, half_rows, features)

    own, send = pl.pallas_call(
        up_kernel,
        out_shape=(
            jax.ShapeDtypeStruct((4, half_rows, 2 * units), jnp.float32),
            jax.ShapeDtypeStruct((4, half_rows, 2 * units), jnp.bfloat16),
        ),
        in_specs=[VMEM] * 5,
        out_specs=(VMEM, VMEM),
        compiler_params=PARAMS,
    )(x, same, w1, w2, w3)
    got = exchange(send, "seq", 1)
    hidden = pl.pallas_call(
        hidden_kernel,
        out_shape=jax.ShapeDtypeStruct((4, half_rows, units), jnp.bfloat16),
        in_specs=[VMEM] * 2,
        out_specs=VMEM,
        compiler_params=PARAMS,
    )(own, got)
    other_hidden = exchange(hidden, "seq", 3)
    partial_out = pl.pallas_call(
        down_kernel,
        out_shape=jax.ShapeDtypeStruct((rows_total, columns), jnp.bfloat16),
        in_specs=[SMEM, VMEM, VMEM, VMEM],
        out_specs=VMEM,
        scratch_shapes=[pltpu.VMEM((rows_total, 4 * units), jnp.bfloat16)],
        compiler_params=PARAMS,
    )(jnp.stack([q, b]).astype(jnp.int32), hidden, other_hidden, down_weight[0])

    returned = lax.all_to_all(
        partial_out.reshape(experts, capacity, columns), "expert", split_axis=0, concat_axis=0, tiled=True
    ).reshape(rows_total, columns)
    mixed = pl.pallas_call(
        mix_kernel,
        out_shape=jax.ShapeDtypeStruct((tok_rows, columns), jnp.bfloat16),
        in_specs=[VMEM] * 3,
        out_specs=VMEM,
        compiler_params=PARAMS,
    )(returned, mixing_high, mixing_low)
    part = tok_rows // sections
    terms = lax.all_to_all(
        mixed.reshape(sections, part, columns), "section", split_axis=0, concat_axis=0, tiled=True
    )
    copies = pl.pallas_call(
        sum_kernel,
        out_shape=jax.ShapeDtypeStruct((sections, part, columns), jnp.bfloat16),
        in_specs=[VMEM],
        out_specs=VMEM,
        compiler_params=PARAMS,
    )(terms)
    return lax.all_to_all(copies, "section", split_axis=0, concat_axis=0, tiled=True).reshape(tok_rows, columns)


def solution(mesh):
    in_specs = (
        P("expert", "section"),
        P("expert", None),
        P("expert", None),
        P("expert", None, ("section", "seq")),
        P("expert", None, ("section", "seq")),
        P("expert", "section", "seq"),
    )
    out_specs = P("expert", "seq")
    return jax.shard_map(shards, mesh=mesh, in_specs=in_specs, out_specs=out_specs, check_vma=False)
```

```python
import jax
import jax.numpy as jnp
from jax import lax
from jax.experimental import pallas as pl
from jax.experimental.pallas import tpu as pltpu
from jax.sharding import PartitionSpec as P

VMEM = pl.BlockSpec(memory_space=pltpu.VMEM)
ANY = pl.BlockSpec(memory_space=pl.ANY)
SMEM = pl.BlockSpec(memory_space=pltpu.SMEM)
PARAMS = pltpu.CompilerParams(vmem_limit_bytes=40 * 1024 * 1024)


def front_kernel(
    which_ref, ids_ref, tokens_ref, gate_ref, up_ref, same_ref, other_ref, rows_ref, place_ref, stage_ref, in_sems, out_sems
):
    units, features = gate_ref.shape[3], gate_ref.shape[2]
    which = which_ref[0]
    copies = [
        pltpu.make_async_copy(
            ref.at[:, which ^ turn], stage_ref.at[turn, :, :, k * units : (k + 1) * units], in_sems.at[2 * turn + k]
        )
        for turn in (1, 0)
        for k, ref in enumerate((gate_ref, up_ref))
    ]
    for copy in copies:
        copy.start()

    experts = which_ref.shape[0]
    top_count, count = ids_ref.shape
    rows_total = rows_ref.shape[0]
    capacity = rows_total // experts
    expert = lax.broadcasted_iota(jnp.int32, (experts, count), 0)
    ids = [ids_ref[k : k + 1, :] for k in range(top_count)]
    named = [jnp.where(expert == i, 1.0, 0.0) for i in ids]
    before = lax.broadcasted_iota(jnp.int32, (count, count), 0) < lax.broadcasted_iota(jnp.int32, (count, count), 1)
    earlier = jnp.dot(
        sum(named).astype(jnp.bfloat16),
        jnp.where(before, 1.0, 0.0).astype(jnp.bfloat16),
        preferred_element_type=jnp.float32,
    )
    row = lax.broadcasted_iota(jnp.int32, (rows_total, count), 0)
    dispatch = jnp.zeros((rows_total, count), jnp.float32)
    for k in range(top_count):
        slot = jnp.sum(named[k] * earlier, axis=0, keepdims=True).astype(jnp.int32)
        place = ids[k] * capacity + slot
        place_ref[k : k + 1, :] = place
        dispatch = dispatch + jnp.where(row == place, 1.0, 0.0)
    mine = tokens_ref[:, pl.ds(pl.multiple_of(which * features, features), features)]
    rows_ref[...] = jnp.dot(dispatch.astype(jnp.bfloat16), mine, preferred_element_type=jnp.float32).astype(jnp.bfloat16)

    outs = [
        pltpu.make_async_copy(stage_ref.at[turn], ref, out_sems.at[turn]) for turn, ref in ((1, other_ref), (0, same_ref))
    ]
    for k, out in enumerate(outs):
        copies[2 * k].wait()
        copies[2 * k + 1].wait()
        out.start()
    for out in outs:
        out.wait()


def up_kernel(x_ref, w0_ref, w1_ref, w2_ref, w3_ref, own_ref, send_ref):
    sections, _, width = x_ref.shape
    for block, w_ref in enumerate((w0_ref, w1_ref, w2_ref, w3_ref)):
        total = None
        for s in range(0, sections, 2):
            rows = jnp.concatenate([x_ref[s], x_ref[s + 1]], axis=1)
            term = jnp.dot(rows, w_ref[s * width : (s + 2) * width, :], preferred_element_type=jnp.float32)
            total = term if total is None else total + term
        own_ref[block] = total
        send_ref[block] = total.astype(jnp.bfloat16)


def hidden_kernel(own_ref, got_ref, out_ref):
    units = out_ref.shape[2]
    for block in range(4):
        total = own_ref[block] + got_ref[block ^ 1].astype(jnp.float32)
        gate, up = total[:, :units], total[:, units:]
        out_ref[block] = (gate / (1.0 + jnp.exp(-gate)) * up).astype(jnp.bfloat16)


def down_kernel(place_ref, own_ref, got_ref, down_ref, out_ref, lhs_ref):
    rows, units = own_ref.shape[1:]
    q, b = place_ref[0], place_ref[1]
    for ref, swap, turn in ((own_ref, (0, 1, 3, 2), 0), (got_ref, (3, 2, 0, 1), 1)):
        row = pl.multiple_of((b ^ turn) * rows, rows)
        for block in range(4):
            unit = pl.multiple_of((q ^ swap[block]) * units, units)
            lhs_ref[pl.ds(row, rows), pl.ds(unit, units)] = ref[block]
    out_ref[...] = jnp.dot(lhs_ref[...], down_ref[...], preferred_element_type=jnp.float32).astype(jnp.bfloat16)


def mix_kernel(returned_ref, high_ref, low_ref, out_ref):
    rows = returned_ref[...]
    out_ref[...] = (
        jnp.dot(high_ref[...], rows, preferred_element_type=jnp.float32)
        + jnp.dot(low_ref[...], rows, preferred_element_type=jnp.float32)
    ).astype(jnp.bfloat16)


def sum_kernel(terms_ref, out_ref):
    total = terms_ref[0].astype(jnp.float32)
    for s in range(1, terms_ref.shape[0]):
        total = total + terms_ref[s].astype(jnp.float32)
    total = total.astype(jnp.bfloat16)
    for s in range(out_ref.shape[0]):
        out_ref[s] = total


def exchange(value, axis, flip):
    return lax.ppermute(value, axis, [(i, i ^ flip) for i in range(lax.axis_size(axis))])


def shards(tokens, route_ids, route_weights, gate_weight, up_weight, down_weight):
    experts, sections = lax.axis_size("expert"), lax.axis_size("section")
    tok_rows, top_count = route_ids.shape
    capacity = 3 * tok_rows * top_count // (2 * experts)
    rows_total = experts * capacity
    features = tokens.shape[1] // 2
    units, columns = gate_weight.shape[2], down_weight.shape[2]
    q = lax.axis_index("seq")
    a, b = (q ^ (q >> 1)) & 1, q >> 1

    shape = jax.ShapeDtypeStruct((sections, features, 2 * units), jnp.bfloat16)
    same, other, outgoing, destination = pl.pallas_call(
        front_kernel,
        out_shape=(
            shape,
            shape,
            jax.ShapeDtypeStruct((rows_total, features), jnp.bfloat16),
            jax.ShapeDtypeStruct((top_count, tok_rows), jnp.int32),
        ),
        in_specs=[SMEM, VMEM, VMEM, ANY, ANY],
        out_specs=(ANY, ANY, VMEM, VMEM),
        scratch_shapes=[
            pltpu.VMEM((2, sections, features, 2 * units), jnp.bfloat16),
            pltpu.SemaphoreType.DMA((4,)),
            pltpu.SemaphoreType.DMA((2,)),
        ],
    )(
        jnp.broadcast_to(a.astype(jnp.int32), (experts,)),
        route_ids.T,
        tokens,
        gate_weight[0].reshape(sections, 2, features, units),
        up_weight[0].reshape(sections, 2, features, units),
    )
    same, other = (w.reshape(sections * features, 2 * units) for w in (same, other))
    w1 = exchange(other, "seq", 1)
    w2 = exchange(same, "seq", 3)
    w3 = exchange(other, "seq", 2)

    place = jnp.arange(rows_total, dtype=jnp.int32)
    named = [destination[k] for k in range(top_count)]
    mixing = sum(
        jnp.where(d[:, None] == place[None, :], route_weights[:, k][:, None], 0.0)
        for k, d in enumerate(named)
    )
    mixing_high = mixing.astype(jnp.bfloat16)
    mixing_low = (mixing - mixing_high.astype(jnp.float32)).astype(jnp.bfloat16)

    received = lax.all_to_all(
        outgoing.reshape(experts, capacity, features), "expert", split_axis=0, concat_axis=0, tiled=True
    )
    half_rows = rows_total // 2
    kept = lax.dynamic_slice_in_dim(received.reshape(rows_total, features), b * half_rows, half_rows, 0)
    kept, mixing_high, mixing_low = lax.optimization_barrier((kept, mixing_high, mixing_low))
    x = lax.all_gather(kept, "section", axis=0, tiled=True).reshape(sections, half_rows, features)

    own, send = pl.pallas_call(
        up_kernel,
        out_shape=(
            jax.ShapeDtypeStruct((4, half_rows, 2 * units), jnp.float32),
            jax.ShapeDtypeStruct((4, half_rows, 2 * units), jnp.bfloat16),
        ),
        in_specs=[VMEM] * 5,
        out_specs=(VMEM, VMEM),
        compiler_params=PARAMS,
    )(x, same, w1, w2, w3)
    got = exchange(send, "seq", 1)
    hidden = pl.pallas_call(
        hidden_kernel,
        out_shape=jax.ShapeDtypeStruct((4, half_rows, units), jnp.bfloat16),
        in_specs=[VMEM] * 2,
        out_specs=VMEM,
        compiler_params=PARAMS,
    )(own, got)
    other_hidden = exchange(hidden, "seq", 3)
    partial_out = pl.pallas_call(
        down_kernel,
        out_shape=jax.ShapeDtypeStruct((rows_total, columns), jnp.bfloat16),
        in_specs=[SMEM, VMEM, VMEM, VMEM],
        out_specs=VMEM,
        scratch_shapes=[pltpu.VMEM((rows_total, 4 * units), jnp.bfloat16)],
        compiler_params=PARAMS,
    )(jnp.stack([q, b]).astype(jnp.int32), hidden, other_hidden, down_weight[0])

    returned = lax.all_to_all(
        partial_out.reshape(experts, capacity, columns), "expert", split_axis=0, concat_axis=0, tiled=True
    ).reshape(rows_total, columns)
    mixed = pl.pallas_call(
        mix_kernel,
        out_shape=jax.ShapeDtypeStruct((tok_rows, columns), jnp.bfloat16),
        in_specs=[VMEM] * 3,
        out_specs=VMEM,
        compiler_params=PARAMS,
    )(returned, mixing_high, mixing_low)
    part = tok_rows // sections
    terms = lax.all_to_all(
        mixed.reshape(sections, part, columns), "section", split_axis=0, concat_axis=0, tiled=True
    )
    copies = pl.pallas_call(
        sum_kernel,
        out_shape=jax.ShapeDtypeStruct((sections, part, columns), jnp.bfloat16),
        in_specs=[VMEM],
        out_specs=VMEM,
        compiler_params=PARAMS,
    )(terms)
    return lax.all_to_all(copies, "section", split_axis=0, concat_axis=0, tiled=True).reshape(tok_rows, columns)


def solution(mesh):
    in_specs = (
        P("expert", "section"),
        P("expert", None),
        P("expert", None),
        P("expert", None, ("section", "seq")),
        P("expert", None, ("section", "seq")),
        P("expert", "section", "seq"),
    )
    out_specs = P("expert", "seq")
    return jax.shard_map(shards, mesh=mesh, in_specs=in_specs, out_specs=out_specs, check_vma=False)
```

```python
import functools

import jax
import jax.numpy as jnp
from jax import lax
from jax.experimental import pallas as pl
from jax.experimental.pallas import tpu as pltpu
from jax.sharding import PartitionSpec as P

VMEM = pl.BlockSpec(memory_space=pltpu.VMEM)
ANY = pl.BlockSpec(memory_space=pl.ANY)
SMEM = pl.BlockSpec(memory_space=pltpu.SMEM)
PARAMS = pltpu.CompilerParams(vmem_limit_bytes=40 * 1024 * 1024)


def split_kernel(which_ref, gate_ref, up_ref, same_ref, other_ref, sems):
    copies = [
        pltpu.make_async_copy(ref.at[:, which_ref[0] ^ turn], out_ref.at[k], sems.at[2 * turn + k])
        for out_ref, turn in ((other_ref, 1), (same_ref, 0))
        for k, ref in enumerate((gate_ref, up_ref))
    ]
    for copy in copies:
        copy.start()
    for copy in copies:
        copy.wait()


def route_kernel(experts, which_ref, ids_ref, tokens_ref, rows_ref, place_ref):
    top_count, count = ids_ref.shape
    rows_total = rows_ref.shape[0]
    capacity = rows_total // experts
    features = tokens_ref.shape[1] // 2
    expert = lax.broadcasted_iota(jnp.int32, (experts, count), 0)
    ids = [ids_ref[k : k + 1, :] for k in range(top_count)]
    named = [jnp.where(expert == i, 1.0, 0.0) for i in ids]
    before = lax.broadcasted_iota(jnp.int32, (count, count), 0) < lax.broadcasted_iota(jnp.int32, (count, count), 1)
    earlier = jnp.dot(
        sum(named).astype(jnp.bfloat16),
        jnp.where(before, 1.0, 0.0).astype(jnp.bfloat16),
        preferred_element_type=jnp.float32,
    )
    row = lax.broadcasted_iota(jnp.int32, (rows_total, count), 0)
    dispatch = jnp.zeros((rows_total, count), jnp.float32)
    for k in range(top_count):
        slot = jnp.sum(named[k] * earlier, axis=0, keepdims=True).astype(jnp.int32)
        place = ids[k] * capacity + slot
        place_ref[k : k + 1, :] = place
        dispatch = dispatch + jnp.where(row == place, 1.0, 0.0)
    mine = tokens_ref[:, pl.ds(pl.multiple_of(which_ref[0] * features, features), features)]
    rows_ref[...] = jnp.dot(dispatch.astype(jnp.bfloat16), mine, preferred_element_type=jnp.float32).astype(jnp.bfloat16)


def up_kernel(x_ref, w0_ref, w1_ref, w2_ref, w3_ref, own_ref, send_ref):
    sections, _, width = x_ref.shape
    for block, w_ref in enumerate((w0_ref, w1_ref, w2_ref, w3_ref)):
        total = None
        for s in range(0, sections, 2):
            rows = jnp.concatenate([x_ref[s], x_ref[s + 1]], axis=1)
            depth = slice(s * width, (s + 2) * width)
            both = jnp.concatenate([w_ref[0, depth, :], w_ref[1, depth, :]], axis=1)
            term = jnp.dot(rows, both, preferred_element_type=jnp.float32)
            total = term if total is None else total + term
        own_ref[block] = total
        send_ref[block] = total.astype(jnp.bfloat16)


def hidden_kernel(own_ref, got_ref, out_ref):
    units = out_ref.shape[2]
    for block in range(4):
        total = own_ref[block] + got_ref[block ^ 1].astype(jnp.float32)
        gate, up = total[:, :units], total[:, units:]
        out_ref[block] = (gate / (1.0 + jnp.exp(-gate)) * up).astype(jnp.bfloat16)


def down_kernel(place_ref, own_ref, got_ref, down_ref, out_ref, lhs_ref):
    rows, units = own_ref.shape[1:]
    q, b = place_ref[0], place_ref[1]
    for ref, swap, turn in ((own_ref, (0, 1, 3, 2), 0), (got_ref, (3, 2, 0, 1), 1)):
        row = pl.multiple_of((b ^ turn) * rows, rows)
        for block in range(4):
            unit = pl.multiple_of((q ^ swap[block]) * units, units)
            lhs_ref[pl.ds(row, rows), pl.ds(unit, units)] = ref[block]
    out_ref[...] = jnp.dot(lhs_ref[...], down_ref[...], preferred_element_type=jnp.float32).astype(jnp.bfloat16)


def mix_kernel(returned_ref, high_ref, low_ref, out_ref):
    rows = returned_ref[...]
    out_ref[...] = (
        jnp.dot(high_ref[...], rows, preferred_element_type=jnp.float32)
        + jnp.dot(low_ref[...], rows, preferred_element_type=jnp.float32)
    ).astype(jnp.bfloat16)


def sum_kernel(terms_ref, out_ref):
    total = terms_ref[0].astype(jnp.float32)
    for s in range(1, terms_ref.shape[0]):
        total = total + terms_ref[s].astype(jnp.float32)
    total = total.astype(jnp.bfloat16)
    for s in range(out_ref.shape[0]):
        out_ref[s] = total


def exchange(value, axis, flip):
    return lax.ppermute(value, axis, [(i, i ^ flip) for i in range(lax.axis_size(axis))])


def shards(tokens, route_ids, route_weights, gate_weight, up_weight, down_weight):
    experts, sections = lax.axis_size("expert"), lax.axis_size("section")
    tok_rows, top_count = route_ids.shape
    capacity = 3 * tok_rows * top_count // (2 * experts)
    rows_total = experts * capacity
    features = tokens.shape[1] // 2
    units, columns = gate_weight.shape[2], down_weight.shape[2]
    q = lax.axis_index("seq")
    a, b = (q ^ (q >> 1)) & 1, q >> 1

    which = a.astype(jnp.int32).reshape(1)
    shape = jax.ShapeDtypeStruct((2, sections, features, units), jnp.bfloat16)
    same, other = pl.pallas_call(
        split_kernel,
        out_shape=(shape, shape),
        in_specs=[SMEM, ANY, ANY],
        out_specs=(VMEM, VMEM),
        scratch_shapes=[pltpu.SemaphoreType.DMA((4,))],
    )(
        which,
        gate_weight[0].reshape(sections, 2, features, units),
        up_weight[0].reshape(sections, 2, features, units),
    )
    same, other = (w.reshape(2, sections * features, units) for w in (same, other))
    w1 = exchange(other, "seq", 1)
    w2 = exchange(same, "seq", 3)
    w3 = exchange(other, "seq", 2)

    outgoing, destination = pl.pallas_call(
        functools.partial(route_kernel, experts),
        out_shape=(
            jax.ShapeDtypeStruct((rows_total, features), jnp.bfloat16),
            jax.ShapeDtypeStruct((top_count, tok_rows), jnp.int32),
        ),
        in_specs=[SMEM, VMEM, VMEM],
        out_specs=(VMEM, VMEM),
        compiler_params=PARAMS,
    )(which, route_ids.T, tokens)
    place = jnp.arange(rows_total, dtype=jnp.int32)
    named = [destination[k] for k in range(top_count)]
    mixing = sum(
        jnp.where(d[:, None] == place[None, :], route_weights[:, k][:, None], 0.0)
        for k, d in enumerate(named)
    )
    mixing_high = mixing.astype(jnp.bfloat16)
    mixing_low = (mixing - mixing_high.astype(jnp.float32)).astype(jnp.bfloat16)

    received = lax.all_to_all(
        outgoing.reshape(experts, capacity, features), "expert", split_axis=0, concat_axis=0, tiled=True
    )
    half_rows = rows_total // 2
    kept = lax.dynamic_slice_in_dim(received.reshape(rows_total, features), b * half_rows, half_rows, 0)
    kept, mixing_high, mixing_low = lax.optimization_barrier((kept, mixing_high, mixing_low))
    x = lax.all_gather(kept, "section", axis=0, tiled=True).reshape(sections, half_rows, features)

    own, send = pl.pallas_call(
        up_kernel,
        out_shape=(
            jax.ShapeDtypeStruct((4, half_rows, 2 * units), jnp.float32),
            jax.ShapeDtypeStruct((4, half_rows, 2 * units), jnp.bfloat16),
        ),
        in_specs=[VMEM] * 5,
        out_specs=(VMEM, VMEM),
        compiler_params=PARAMS,
    )(x, same, w1, w2, w3)
    got = exchange(send, "seq", 1)
    hidden = pl.pallas_call(
        hidden_kernel,
        out_shape=jax.ShapeDtypeStruct((4, half_rows, units), jnp.bfloat16),
        in_specs=[VMEM] * 2,
        out_specs=VMEM,
        compiler_params=PARAMS,
    )(own, got)
    other_hidden = exchange(hidden, "seq", 3)
    partial_out = pl.pallas_call(
        down_kernel,
        out_shape=jax.ShapeDtypeStruct((rows_total, columns), jnp.bfloat16),
        in_specs=[SMEM, VMEM, VMEM, VMEM],
        out_specs=VMEM,
        scratch_shapes=[pltpu.VMEM((rows_total, 4 * units), jnp.bfloat16)],
        compiler_params=PARAMS,
    )(jnp.stack([q, b]).astype(jnp.int32), hidden, other_hidden, down_weight[0])

    returned = lax.all_to_all(
        partial_out.reshape(experts, capacity, columns), "expert", split_axis=0, concat_axis=0, tiled=True
    ).reshape(rows_total, columns)
    mixed = pl.pallas_call(
        mix_kernel,
        out_shape=jax.ShapeDtypeStruct((tok_rows, columns), jnp.bfloat16),
        in_specs=[VMEM] * 3,
        out_specs=VMEM,
        compiler_params=PARAMS,
    )(returned, mixing_high, mixing_low)
    part = tok_rows // sections
    terms = lax.all_to_all(
        mixed.reshape(sections, part, columns), "section", split_axis=0, concat_axis=0, tiled=True
    )
    copies = pl.pallas_call(
        sum_kernel,
        out_shape=jax.ShapeDtypeStruct((sections, part, columns), jnp.bfloat16),
        in_specs=[VMEM],
        out_specs=VMEM,
        compiler_params=PARAMS,
    )(terms)
    return lax.all_to_all(copies, "section", split_axis=0, concat_axis=0, tiled=True).reshape(tok_rows, columns)


def solution(mesh):
    in_specs = (
        P("expert", "section"),
        P("expert", None),
        P("expert", None),
        P("expert", None, ("section", "seq")),
        P("expert", None, ("section", "seq")),
        P("expert", "section", "seq"),
    )
    out_specs = P("expert", "seq")
    return jax.shard_map(shards, mesh=mesh, in_specs=in_specs, out_specs=out_specs, check_vma=False)
```
